32 devices in a mesh: gx: 4 (over z), gy: 8 (over y, x, core).
Axes of the slice: x: 2, y: 2, z: 4, core: 2. Of those that a mesh axis runs over, the one named last changes fastest.
Arguments:
- tokens: bfloat16 [2, 12288, 1024], P(None, ('gx', 'gy')), may hold values from -6 to 6
- cotangent: bfloat16 [2, 12288, 1024], P(None, ('gx', 'gy')), may hold values from -6 to 6
- image_ids: int32 [2, 8, 1536], P(None, 'gy'), may hold values from 0 to 2, as said below
- block_layout: int32 [2, 8, 12], P(None, 'gy'), may hold values from 0 to 11, as said below
- qkv_weight: bfloat16 [1024, 3072], P(('gx', 'gy')), may hold values from -0.1875 to 0.1875
- out_weight: bfloat16 [1024, 1024], P(('gx', 'gy')), may hold values from -6 to 6
- up_weight: bfloat16 [1024, 4096], P(('gx', 'gy')), may hold values from -0.1875 to 0.1875
- down_weight: bfloat16 [4096, 1024], P(('gx', 'gy')), may hold values from -0.09375 to 0.09375
- attn_gain: bfloat16 [1024], P(('gx', 'gy')), may hold values from 0.5 to 1.5
- attn_shift: bfloat16 [1024], P(('gx', 'gy')), may hold values from -3 to 3
- query_bias: bfloat16 [1024], P(('gx', 'gy')), may hold values from -3 to 3
- value_bias: bfloat16 [1024], P(('gx', 'gy')), may hold values from -3 to 3
- out_bias: bfloat16 [1024], P(('gx', 'gy')), may hold values from -3 to 3
- attn_scale: bfloat16 [1024], P(('gx', 'gy')), may hold values from 0.5 to 1.5
- mlp_gain: bfloat16 [1024], P(('gx', 'gy')), may hold values from 0.5 to 1.5
- mlp_shift: bfloat16 [1024], P(('gx', 'gy')), may hold values from -3 to 3
- up_bias: bfloat16 [4096], P(('gx', 'gy')), may hold values from -3 to 3
- down_bias: bfloat16 [1024], P(('gx', 'gy')), may hold values from -3 to 3
- mlp_scale: bfloat16 [1024], P(('gx', 'gy')), may hold values from 0.5 to 1.5
Outputs:
- block_out: bfloat16 [2, 12288, 1024], P(None, ('gx', 'gy'))
- token_grad: bfloat16 [2, 12288, 1024], P(None, ('gx', 'gy'))
- qkv_weight_grad: float32 [1024, 3072], P(('gx', 'gy'))
- out_weight_grad: float32 [1024, 1024], P(('gx', 'gy'))
- up_weight_grad: float32 [1024, 4096], P(('gx', 'gy'))
- down_weight_grad: float32 [4096, 1024], P(('gx', 'gy'))
- attn_gain_grad: float32 [1024], P(('gx', 'gy'))
- attn_shift_grad: float32 [1024], P(('gx', 'gy'))
- query_bias_grad: float32 [1024], P(('gx', 'gy'))
- value_bias_grad: float32 [1024], P(('gx', 'gy'))
- out_bias_grad: float32 [1024], P(('gx', 'gy'))
- attn_scale_grad: float32 [1024], P(('gx', 'gy'))
- mlp_gain_grad: float32 [1024], P(('gx', 'gy'))
- mlp_shift_grad: float32 [1024], P(('gx', 'gy'))
- up_bias_grad: float32 [4096], P(('gx', 'gy'))
- down_bias_grad: float32 [1024], P(('gx', 'gy'))
- mlp_scale_grad: float32 [1024], P(('gx', 'gy'))
The draws below stay inside these ranges and needn't reach their ends.
Inputs may be any that keep to these rules, and one draw needn't show every extreme that they name: `image_ids`: along each pack (one micro-batch, one column) ids start at 0, never fall and rise by one at each new image; each image covers 1 to 1370 consecutive positions, image 1 covers exactly 1370, and the last image ends at the pack's end. `block_layout`: entry d * 3 + s of a micro-batch and column is s * 4 + ((d + r) mod 4), with one turn r of 0 to 3 for each micro-batch and column.
All inputs are finite; a program needn't handle non-finite values.
Results may differ from the reference program's by a relative error of at most 0.018.
Values may be sent and summed in bfloat16 or wider, within the bound.
A program may use at most 448 MiB of HBM per device.

```python
import math
import jax
import jax.numpy as jnp
from jax import lax

D = 1024
HEADS = 16
HEAD_DIM = 64
FF = 4096
IMG_TOK = 1370
BLOCK = 128
MICRO = 2
TOK_MB = 384
COLUMN_DEVS = 4
COLUMNS = 8
PACK = 1536
BLK_DEV = 3
BLK_PACK = 12
TOKENS = 12288
N_GX = 4
N_GY = 8


def draw_image_ids(key, part):
    key = jax.random.fold_in(key, 11)
    rest_count = (PACK - IMG_TOK - 1) // (IMG_TOK // 2) + 1
    lead_top = min(IMG_TOK, PACK - IMG_TOK - rest_count)
    leading = jax.random.randint(key, (MICRO, COLUMNS, 1), 1, lead_top + 1).astype(jnp.int32)
    remaining = PACK - IMG_TOK - leading
    share = remaining // rest_count
    extra = remaining - share * rest_count
    slots = jnp.arange(rest_count, dtype=jnp.int32)
    base = share + (slots[None, None, :] < extra).astype(jnp.int32)
    shift_key = jax.random.fold_in(key, 1)
    raw = jax.random.randint(shift_key, (MICRO, COLUMNS, rest_count + 1), 0, 1 << 20).astype(jnp.int32)
    moves = raw % (share // 2 + 1)
    edges = jnp.arange(rest_count + 1, dtype=jnp.int32)
    inner = ((edges > 0) & (edges < rest_count)).astype(jnp.int32)
    moves = moves * inner[None, None, :]
    rest_lengths = base + moves[..., 1:] - moves[..., :-1]
    largest = jnp.full((MICRO, COLUMNS, 1), IMG_TOK, jnp.int32)
    lengths = jnp.concatenate([leading, largest, rest_lengths], axis=-1).astype(jnp.int32)
    ends = jnp.cumsum(lengths, axis=-1).astype(jnp.int32)
    positions = jnp.arange(PACK, dtype=jnp.int32)
    passed = (ends[..., None, :] <= positions[:, None]).astype(jnp.int32)
    return jnp.sum(passed, axis=-1).astype(jnp.int32)


def draw_block_layout(key, part):
    key = jax.random.fold_in(key, 23)
    turns = jax.random.randint(key, (MICRO, COLUMNS, 1), 0, COLUMN_DEVS)
    places = jnp.arange(BLK_PACK, dtype=jnp.int32)
    device_of = places // BLK_DEV
    within = places % BLK_DEV
    return (within * COLUMN_DEVS + (device_of + turns) % COLUMN_DEVS).astype(jnp.int32)


def block_scale(key, dims, shards, low, high):
    level = 1.0
    for axis_at, blocks in shards:
        steps = jax.random.uniform(jax.random.fold_in(jax.random.fold_in(key, 6), axis_at), (blocks,), jnp.float32, low / len(shards), high / len(shards))
        level = level * jnp.repeat(jnp.exp(steps), dims[axis_at] // blocks).reshape((-1,) + (1,) * (len(dims) - 1 - axis_at))
    return level


def gaussian(stream_key, dims, scale, most, cuts=(), kind=jnp.bfloat16):
    factor_of = block_scale(stream_key, dims, cuts, -0.22, 0.18) if cuts else 1.0
    entries = jax.random.normal(stream_key, dims, jnp.float32) * scale * factor_of
    return jnp.minimum(jnp.maximum(entries, -most), most).astype(kind)


def setup_inputs(seed: int = 0) -> dict:
    streams_of = jax.random.split(jax.random.key(seed), 20)
    return {
        "tokens": gaussian(streams_of[0], (MICRO, TOKENS, D), 1.0, 6.0, ((1, 32),)),
        "cotangent": gaussian(streams_of[1], (MICRO, TOKENS, D), 1.0, 6.0, ((1, 32),)),
        "image_ids": draw_image_ids(jax.random.fold_in(streams_of[19], 71), 0),
        "block_layout": draw_block_layout(jax.random.fold_in(streams_of[19], 71), 0),
        "qkv_weight": gaussian(streams_of[4], (D, 3 * D), D ** -0.5, 0.1875, ((0, 32),)),
        "out_weight": gaussian(streams_of[5], (D, D), (max(1, (2 * D) // IMG_TOK)) ** -0.5, 6.0, ((0, 32),)),
        "up_weight": gaussian(streams_of[6], (D, FF), D ** -0.5, 0.1875, ((0, 32),)),
        "down_weight": gaussian(streams_of[7], (FF, D), FF ** -0.5, 0.09375, ((0, 32),)),
        "attn_gain": jnp.clip(0.5 + 1.0 * jax.random.uniform(streams_of[8], (D,), jnp.float32) ** block_scale(streams_of[8], (D,), ((0, 32),), -0.2, 0.2), 0.5, 1.5).astype(jnp.bfloat16),
        "attn_shift": gaussian(streams_of[9], (D,), 0.5, 3.0, ((0, 32),)),
        "query_bias": gaussian(streams_of[10], (D,), 0.5, 3.0, ((0, 32),)),
        "value_bias": gaussian(streams_of[11], (D,), 0.5, 3.0, ((0, 32),)),
        "out_bias": gaussian(streams_of[12], (D,), 0.5, 3.0, ((0, 32),)),
        "attn_scale": jnp.clip(0.5 + 1.0 * jax.random.uniform(streams_of[13], (D,), jnp.float32) ** block_scale(streams_of[13], (D,), ((0, 32),), -0.2, 0.2), 0.5, 1.5).astype(jnp.bfloat16),
        "mlp_gain": jnp.clip(0.5 + 1.0 * jax.random.uniform(streams_of[14], (D,), jnp.float32) ** block_scale(streams_of[14], (D,), ((0, 32),), -0.2, 0.2), 0.5, 1.5).astype(jnp.bfloat16),
        "mlp_shift": gaussian(streams_of[15], (D,), 0.5, 3.0, ((0, 32),)),
        "up_bias": gaussian(streams_of[16], (FF,), 0.5, 3.0, ((0, 32),)),
        "down_bias": gaussian(streams_of[17], (D,), 0.5, 3.0, ((0, 32),)),
        "mlp_scale": jnp.clip(0.5 + 1.0 * jax.random.uniform(streams_of[18], (D,), jnp.float32) ** block_scale(streams_of[18], (D,), ((0, 32),), -0.2, 0.2), 0.5, 1.5).astype(jnp.bfloat16),
    }


EPS = 1e-06

@jax.custom_vjp
def low(v):
    return lax.optimization_barrier(v.astype(jnp.bfloat16)).astype(jnp.float32)

@jax.custom_vjp
def low_back(v):
    return v

def low_keep(v):
    return (low(v), None)

def low_pass(kept, grad):
    return (grad,)

def back_keep(v):
    return (v, None)

def back_low(kept, grad):
    return (low(grad),)
low.defvjp(low_keep, low_pass)
low_back.defvjp(back_keep, back_low)

def matmul(left, right):
    return jnp.dot(left, right, precision=lax.Precision.HIGHEST)

def layer_norm(rows, gain, shift):
    mean_row = lax.optimization_barrier(jnp.mean(rows, axis=-1, keepdims=True))
    centered = rows - mean_row
    variance = lax.optimization_barrier(jnp.mean(centered * centered, axis=-1, keepdims=True))
    return centered * lax.rsqrt(variance + EPS) * gain + shift

def attend_block(query_block, id_block, key_rows, value_rows, id_rows):
    block_rows = query_block.shape[0]
    pack_rows = key_rows.shape[0]
    query_heads = query_block.reshape(block_rows, HEADS, HEAD_DIM)
    key_heads = key_rows.reshape(pack_rows, HEADS, HEAD_DIM)
    value_heads = value_rows.reshape(pack_rows, HEADS, HEAD_DIM)
    raw_scores = jnp.einsum('qhd,khd->hqk', query_heads, key_heads, precision=lax.Precision.HIGHEST) * HEAD_DIM ** (-0.5)
    raw_scores = low_back(raw_scores)
    same_image = id_block[:, None] == id_rows[None, :]
    masked = jnp.where(same_image[None], raw_scores, -jnp.inf)
    top_score = lax.optimization_barrier(jnp.max(masked, axis=-1, keepdims=True))
    expo_scores = jnp.exp(masked - top_score)
    weights = low(expo_scores / lax.optimization_barrier(jnp.sum(expo_scores, axis=-1, keepdims=True)))
    merged = jnp.einsum('hqk,khd->qhd', weights, value_heads, precision=lax.Precision.HIGHEST)
    return merged.reshape(block_rows, HEADS * HEAD_DIM)

def attention(query_rows, key_rows, value_rows, id_rows):
    pack_rows = query_rows.shape[0]
    span = math.gcd(pack_rows, 512)
    query_blocks = query_rows.reshape(pack_rows // span, span, query_rows.shape[1])
    id_blocks = id_rows.reshape(pack_rows // span, span)

    def one_block(paired):
        return attend_block(paired[0], paired[1], key_rows, value_rows, id_rows)
    merged = lax.map(jax.checkpoint(one_block), (query_blocks, id_blocks))
    return merged.reshape(pack_rows, query_rows.shape[1])

def pack_layer(x_rows, id_rows, weights_all):
    qkv_w, out_w, up_w, down_w, attn_g, attn_s, query_b, value_b, out_b, attn_ls, mlp_g, mlp_s, up_b, down_b, mlp_ls = weights_all
    width = x_rows.shape[1]
    normed_one = low(layer_norm(x_rows, attn_g, attn_s))
    projected = matmul(normed_one, qkv_w)
    query_rows = low_back(low(projected[:, :width] + query_b))
    key_rows = low_back(low(projected[:, width:2 * width]))
    value_rows = low_back(low(projected[:, 2 * width:] + value_b))
    attended = low_back(low(attention(query_rows, key_rows, value_rows, id_rows)))
    branch_one = low_back(matmul(attended, out_w) + out_b)
    resid = x_rows + attn_ls * branch_one
    normed_two = low(layer_norm(resid, mlp_g, mlp_s))
    hidden = low_back(matmul(normed_two, up_w) + up_b)
    active = low(jax.nn.gelu(hidden, approximate=False))
    branch_two = low_back(matmul(active, down_w) + down_b)
    return resid + mlp_ls * branch_two

def reference(tokens, cotangent, image_ids, block_layout, qkv_weight, out_weight, up_weight, down_weight, attn_gain, attn_shift, query_bias, value_bias, out_bias, attn_scale, mlp_gain, mlp_shift, up_bias, down_bias, mlp_scale):
    params = tuple((arr.astype(jnp.float32) for arr in (qkv_weight, out_weight, up_weight, down_weight, attn_gain, attn_shift, query_bias, value_bias, out_bias, attn_scale, mlp_gain, mlp_shift, up_bias, down_bias, mlp_scale)))
    width = tokens.shape[-1]

    def to_packs(arr):
        shaped = arr.reshape(MICRO, N_GX, N_GY, TOK_MB, width)
        return jnp.transpose(shaped, (0, 2, 1, 3, 4)).reshape(MICRO * N_GY, N_GX * TOK_MB, width)

    def from_packs(arr):
        shaped = arr.reshape(MICRO, N_GY, N_GX, TOK_MB, width)
        return jnp.transpose(shaped, (0, 2, 1, 3, 4)).reshape(MICRO, N_GX * N_GY * TOK_MB, width)
    offsets = jnp.arange(BLOCK, dtype=jnp.int32)
    positions = (block_layout[..., None] * BLOCK + offsets).reshape(MICRO, N_GY, N_GX * TOK_MB).astype(jnp.int32)
    id_packs = jnp.take_along_axis(image_ids, positions, axis=2).reshape(MICRO * N_GY, N_GX * TOK_MB)

    def forward(x_packs, weights_all):

        def one_pack(carried, item):
            return (carried, pack_layer(item[0], item[1], weights_all))
        _, result = lax.scan(one_pack, jnp.zeros((), jnp.float32), (x_packs, id_packs))
        return result
    out_packs, pull = jax.vjp(forward, to_packs(tokens.astype(jnp.float32)), params)
    grad_packs, grads = pull(to_packs(cotangent.astype(jnp.float32)))
    return (from_packs(out_packs).astype(jnp.bfloat16), from_packs(grad_packs).astype(jnp.bfloat16), grads[0], grads[1], grads[2], grads[3], grads[4], grads[5], grads[6], grads[7], grads[8], grads[9], grads[10], grads[11], grads[12], grads[13], grads[14])
```

```python
import functools

import jax
import jax.numpy as jnp
from jax import lax
from jax.experimental import pallas as pl
from jax.experimental.pallas import tpu as pltpu
from jax.sharding import PartitionSpec as P

HEAD_DIM = 64
PAIR = 2 * HEAD_DIM
BLOCK = 128
EPS = 1e-06
MASKED = -1e30
ID_LANES = 8
SCALE = HEAD_DIM ** (-0.5)
LOG2E = 1.4426950408889634
EXP_SCALE = SCALE * LOG2E
AXES = ("gx", "gy")
NT = (((1,), (1,)), ((), ()))
NN = (((1,), (0,)), ((), ()))
VMEM_BYTES = 50 * 1024 * 1024


def dot32(left, right, dims):
    return lax.dot_general(left, right, dims, preferred_element_type=jnp.float32)


def norm_parts(rows, gain, shift):
    mean_row = jnp.mean(rows, axis=-1, keepdims=True)
    centered = rows - mean_row
    inv_std = lax.rsqrt(jnp.mean(centered * centered, axis=-1, keepdims=True) + EPS)
    unit_rows = centered * inv_std
    return (unit_rows * gain + shift, unit_rows, inv_std)


def norm_back(grad_out, unit_rows, inv_std, gain):
    scaled = grad_out * gain
    return inv_std * (
        scaled
        - jnp.mean(scaled, axis=-1, keepdims=True)
        - unit_rows * jnp.mean(scaled * unit_rows, axis=-1, keepdims=True)
    )


def outer_sum(left, right):
    return dot32(left, right, (((0,), (0,)), ((), ())))


def back_dot(grad_rows, weight):
    return dot32(grad_rows, weight, NT)


def lane_of(shape):
    return lax.broadcasted_iota(jnp.int32, shape, len(shape) - 1)


def attend_kernel(group, *refs):
    q_ref, qmask_ref = refs[:2]
    k_refs = refs[2 : 2 + group]
    v_refs = refs[2 + group : 2 + 2 * group]
    mask_refs = refs[2 + 2 * group : 2 + 3 * group]
    out_ref, lse_ref = refs[2 + 3 * group :]
    q = q_ref[...].astype(jnp.float32)
    qmask = qmask_ref[...].astype(jnp.float32)
    first = lane_of(q.shape) < HEAD_DIM
    key_first = lane_of(k_refs[0].shape) < HEAD_DIM
    accs, tops = [], []
    for head in range(2):
        q_head = jnp.where(first == (head == 0), q, qmask).astype(jnp.bfloat16)
        mine = key_first == (head == 0)
        scores = []
        for k_ref, mask_ref in zip(k_refs, mask_refs):
            k_head = jnp.where(
                mine, k_ref[...].astype(jnp.float32), mask_ref[...].astype(jnp.float32)
            ).astype(jnp.bfloat16)
            scores.append(dot32(q_head, k_head, NT))
        top = functools.reduce(
            jnp.maximum, [jnp.max(score, axis=-1, keepdims=True) for score in scores]
        )
        acc = jnp.zeros(q.shape, jnp.float32)
        for score, v_ref in zip(scores, v_refs):
            weights = jnp.exp2((score - top) * EXP_SCALE).astype(jnp.bfloat16)
            v_head = jnp.where(mine, v_ref[...].astype(jnp.float32), 1.0).astype(jnp.bfloat16)
            acc = acc + dot32(weights, v_head, NN)
        accs.append(acc)
        tops.append(top)
    mixed = jnp.where(first, accs[0], accs[1])
    sums = jnp.where(first, accs[1], accs[0])
    out_ref[...] = (mixed / pltpu.roll(sums, HEAD_DIM, 1)).astype(out_ref.dtype)
    lse_ref[...] = jnp.where(first, tops[1], tops[0]) + jnp.log2(sums) * (1.0 / EXP_SCALE)


def attend(qkv_rows, others, query_mask, key_masks):
    rows, width = qkv_rows.shape[0], qkv_rows.shape[1] // 3
    pairs = width // PAIR
    tile = rows // 2
    group = 1 + len(others)

    def col(offset):
        return pl.BlockSpec((rows, PAIR), lambda j, i: (0, offset * pairs + j))

    whole = pl.BlockSpec((rows, PAIR), lambda j, i: (0, 0))
    tiled = pl.BlockSpec((tile, PAIR), lambda j, i: (i, j))
    cells = 2 * pairs * rows * rows * group
    return pl.pallas_call(
        functools.partial(attend_kernel, group),
        grid=(pairs, 2),
        in_specs=[tiled, pl.BlockSpec((tile, PAIR), lambda j, i: (i, 0))]
        + [col(1)]
        + [col(0)] * (group - 1)
        + [col(2)]
        + [col(1)] * (group - 1)
        + [whole] * group,
        out_specs=[tiled, tiled],
        out_shape=[
            jax.ShapeDtypeStruct((rows, width), jnp.bfloat16),
            jax.ShapeDtypeStruct((rows, width), jnp.float32),
        ],
        compiler_params=pltpu.CompilerParams(vmem_limit_bytes=VMEM_BYTES),
        cost_estimate=pl.CostEstimate(
            flops=cells * 512, bytes_accessed=rows * width * 16, transcendentals=cells
        ),
        name="attend",
    )(qkv_rows, query_mask, qkv_rows, *others, qkv_rows, *others, *key_masks)


def back_kernel(has_prior, *refs):
    q_ref, g_ref, o_ref, lse_ref, qmask_ref, k_ref, v_ref, kmask_ref = refs[:8]
    prior_ref = refs[8] if has_prior else None
    dq_ref, dk_ref, dv_ref = refs[8 + has_prior :]
    q_low, g_low, k_low = q_ref[...], g_ref[...], k_ref[...]
    q = q_low.astype(jnp.float32)
    g = g_low.astype(jnp.float32)
    k = k_low.astype(jnp.float32)
    v = v_ref[...].astype(jnp.float32)
    qmask = qmask_ref[...].astype(jnp.float32)
    kmask = kmask_ref[...].astype(jnp.float32)
    lse = lse_ref[...]
    product = g * o_ref[...].astype(jnp.float32)
    lane = lane_of(q.shape)
    first = lane < HEAD_DIM
    spare = lane % HEAD_DIM
    key_lane = lane_of(k.shape)
    key_first = key_lane < HEAD_DIM
    key_spare = key_lane % HEAD_DIM
    ones = (key_spare >= ID_LANES) & (key_spare < ID_LANES + 3)
    key_fill = jnp.where(ones, -1.0, kmask)
    value_fill = jnp.where(ones, -1.0, 0.0)
    k_turned = k.T.astype(jnp.bfloat16)

    def split(values, rest):
        high = values.astype(jnp.bfloat16).astype(jnp.float32)
        left = values - high
        middle = left.astype(jnp.bfloat16).astype(jnp.float32)
        low = left - middle
        return jnp.where(
            spare == ID_LANES,
            high,
            jnp.where(
                spare == ID_LANES + 1, middle, jnp.where(spare == ID_LANES + 2, low, rest)
            ),
        )

    query_fill = split(lse, qmask)
    delta = [
        jnp.sum(jnp.where(first == (head == 0), product, 0.0), axis=-1, keepdims=True)
        for head in range(2)
    ]
    grad_fill = split(jnp.where(first, delta[1], delta[0]), 0.0)
    dq_turned, dks, dvs = [], [], []
    for head in range(2):
        mine = first == (head == 0)
        key_mine = key_first == (head == 0)
        q_head = jnp.where(mine, q, query_fill).astype(jnp.bfloat16)
        g_head = jnp.where(mine, g, grad_fill).astype(jnp.bfloat16)
        k_head = jnp.where(key_mine, k, key_fill).astype(jnp.bfloat16)
        v_head = jnp.where(key_mine, v, value_fill).astype(jnp.bfloat16)
        probs = jnp.exp2(dot32(k_head, q_head, NT) * EXP_SCALE)
        grads = (probs * dot32(v_head, g_head, NT)).astype(jnp.bfloat16)
        dvs.append(dot32(probs.astype(jnp.bfloat16), g_low, NN))
        dks.append(dot32(grads, q_low, NN))
        dq_turned.append(
            dot32(k_turned[head * HEAD_DIM : (head + 1) * HEAD_DIM], grads, NN)
        )
    dq = jnp.concatenate(dq_turned, axis=0).T * SCALE
    if has_prior:
        dq = dq + prior_ref[...]
    dq_ref[...] = dq.astype(dq_ref.dtype)
    dk_ref[...] = (jnp.where(key_first, dks[0], dks[1]) * SCALE).astype(dk_ref.dtype)
    dv_ref[...] = jnp.where(key_first, dvs[0], dvs[1]).astype(dv_ref.dtype)


def attend_back(
    qkv_rows, grad_mixed, mixed, lse, query_mask, key_value, key_mask, prior, own, last
):
    rows, width = mixed.shape
    pairs = width // PAIR

    def col(offset):
        return pl.BlockSpec((rows, PAIR), lambda j: (0, offset * pairs + j))

    whole = pl.BlockSpec((rows, PAIR), lambda j: (0, 0))
    has_prior = prior is not None
    cells = 2 * pairs * rows * rows
    return pl.pallas_call(
        functools.partial(back_kernel, has_prior),
        grid=(pairs,),
        in_specs=[col(0)] * 4
        + [whole, col(1 if own else 0), col(2 if own else 1), whole]
        + [col(0)] * has_prior,
        out_specs=[col(0)] * 3,
        out_shape=[
            jax.ShapeDtypeStruct((rows, width), jnp.bfloat16 if last else jnp.float32),
            jax.ShapeDtypeStruct((rows, width), jnp.bfloat16),
            jax.ShapeDtypeStruct((rows, width), jnp.bfloat16),
        ],
        compiler_params=pltpu.CompilerParams(vmem_limit_bytes=VMEM_BYTES),
        cost_estimate=pl.CostEstimate(
            flops=cells * 1280, bytes_accessed=rows * width * 20, transcendentals=cells
        ),
        name="attend_back",
    )(
        qkv_rows,
        grad_mixed,
        mixed,
        lse,
        query_mask,
        key_value,
        key_value,
        key_mask,
        *([prior] if has_prior else []),
    )


def gelu_parts(values):
    phi = 0.5 * (1.0 + lax.erf(values * 0.7071067811865476))
    density = 0.3989422804014327 * jnp.exp(-0.5 * values * values)
    return values * phi, phi + values * density


def shards(n_gx, n_gy, tokens, cotangent, image_ids, block_layout, *params):
    qkv_weight, out_weight, up_weight, down_weight = params[:4]
    vectors = params[4:]
    devices = n_gx * n_gy
    chips = n_gx // 4
    group = 2 * chips
    row_count, width = tokens.shape[1:]
    place = lax.axis_index("gx")
    odd = place % 2 == 1

    def linear(line, pack, member):
        return (pack * chips + member // 2) * n_gy + 2 * line + member % 2

    moves = [
        [
            (z * n_gy + 2 * line + core, linear(line, 2 * ((step + z) % 2) + core, z // 2))
            for z in range(n_gx)
            for line in range(n_gy // 2)
            for core in range(2)
        ]
        for step in range(2)
    ]
    rounds = [
        [
            (linear(line, pack, member), linear(line, pack, (member + turn) % group))
            for line in range(n_gy // 2)
            for pack in range(4)
            for member in range(group)
        ]
        for turn in range(1, group)
    ]

    def back(perm):
        return [(target, source) for source, target in perm]

    def to_packs(pair):
        even_first = [jnp.where(odd, pair[1], pair[0]), jnp.where(odd, pair[0], pair[1])]
        return jnp.concatenate(
            [lax.ppermute(part, AXES, moves[step]) for step, part in enumerate(even_first)],
            axis=0,
        )

    def from_packs(rows):
        parts = [
            lax.ppermute(
                rows[step * row_count : (step + 1) * row_count], AXES, back(moves[step])
            )
            for step in range(2)
        ]
        return jnp.stack(
            [jnp.where(odd, parts[1], parts[0]), jnp.where(odd, parts[0], parts[1])]
        )

    def gather(shard):
        return lax.all_gather(shard, AXES, axis=0, tiled=True)

    blocks = row_count // BLOCK
    own_layout = lax.dynamic_slice_in_dim(block_layout[:, 0], place * blocks, blocks, axis=1)
    own_ids = jnp.take_along_axis(
        image_ids[:, 0].reshape(image_ids.shape[0], -1, BLOCK), own_layout[..., None], axis=1
    ).reshape(-1, row_count)

    x_low = to_packs(tokens)
    sizes = [vector.shape[0] for vector in vectors]
    fetched = gather(jnp.concatenate(vectors)[None])
    ends, start = [], 0
    for size in sizes:
        ends.append((start, start + size))
        start += size
    (
        gain_attn,
        shift_attn,
        bias_query,
        bias_value,
        bias_out,
        scale_attn,
        gain_mlp,
        shift_mlp,
        bias_up,
        bias_down,
        scale_mlp,
    ) = [fetched[:, low:high].reshape(-1).astype(jnp.float32) for low, high in ends]
    qkv_w = gather(qkv_weight)
    out_w = gather(out_weight)
    up_w = gather(up_weight)
    down_w = gather(down_weight)

    ids = to_packs(own_ids)
    id_sets = [ids] + [lax.ppermute(ids, AXES, perm) for perm in rounds]
    spare = jnp.arange(PAIR, dtype=jnp.int32)[None, :] % HEAD_DIM
    query_mask = (spare == ids[:, None]).astype(jnp.bfloat16)
    key_masks = [
        jnp.where((spare < ID_LANES) & (spare != each[:, None]), MASKED, 0.0).astype(jnp.bfloat16)
        for each in id_sets
    ]

    x_rows = x_low.astype(jnp.float32)
    normed_one, unit_one, inv_one = norm_parts(x_rows, gain_attn, shift_attn)
    normed_one_low = normed_one.astype(jnp.bfloat16)
    qkv_bias = jnp.concatenate([bias_query, jnp.zeros_like(bias_query), bias_value])
    qkv_rows = (
        jnp.dot(normed_one_low, qkv_w, preferred_element_type=jnp.float32) + qkv_bias
    ).astype(jnp.bfloat16)
    own_kv = qkv_rows[:, width:]
    others = [lax.ppermute(own_kv, AXES, perm) for perm in rounds]
    mixed_low, lse = attend(qkv_rows, others, query_mask, key_masks)
    branch_one = jnp.dot(mixed_low, out_w, preferred_element_type=jnp.float32) + bias_out
    resid = x_rows + scale_attn * branch_one
    normed_two, unit_two, inv_two = norm_parts(resid, gain_mlp, shift_mlp)
    normed_two_low = normed_two.astype(jnp.bfloat16)
    hidden = jnp.dot(normed_two_low, up_w, preferred_element_type=jnp.float32) + bias_up
    active, slope = gelu_parts(hidden)
    active_low = active.astype(jnp.bfloat16)
    branch_two = jnp.dot(active_low, down_w, preferred_element_type=jnp.float32) + bias_down
    block_out = from_packs((resid + scale_mlp * branch_two).astype(jnp.bfloat16))

    def reduce(total):
        return lax.psum_scatter(
            total.astype(jnp.bfloat16), AXES, scatter_dimension=0, tiled=True
        ).astype(jnp.float32)

    grad_y = to_packs(cotangent).astype(jnp.float32)
    d_scale_mlp = jnp.sum(grad_y * branch_two, axis=0)
    grad_two = (scale_mlp * grad_y).astype(jnp.bfloat16)
    d_bias_down = jnp.sum(grad_two.astype(jnp.float32), axis=0)
    d_down = reduce(outer_sum(active_low, grad_two))
    grad_hidden = (back_dot(grad_two, down_w) * slope).astype(jnp.bfloat16)
    d_bias_up = jnp.sum(grad_hidden.astype(jnp.float32), axis=0)
    d_up = reduce(outer_sum(normed_two_low, grad_hidden))
    grad_norm_two = back_dot(grad_hidden, up_w)
    d_gain_mlp = jnp.sum(grad_norm_two * unit_two, axis=0)
    d_shift_mlp = jnp.sum(grad_norm_two, axis=0)
    grad_resid = grad_y + norm_back(grad_norm_two, unit_two, inv_two, gain_mlp)
    d_scale_attn = jnp.sum(grad_resid * branch_one, axis=0)
    grad_one = (scale_attn * grad_resid).astype(jnp.bfloat16)
    d_bias_out = jnp.sum(grad_one.astype(jnp.float32), axis=0)
    d_out = reduce(outer_sum(mixed_low, grad_one))
    grad_mixed = back_dot(grad_one, out_w).astype(jnp.bfloat16)

    prior, returned = None, []
    for perm, key_value, key_mask in zip(rounds, others, key_masks[1:]):
        prior, part_k, part_v = attend_back(
            qkv_rows, grad_mixed, mixed_low, lse, query_mask, key_value, key_mask, prior, False, False
        )
        returned.append(
            (lax.ppermute(part_k, AXES, back(perm)), lax.ppermute(part_v, AXES, back(perm)))
        )
    grad_q, grad_k, grad_v = attend_back(
        qkv_rows, grad_mixed, mixed_low, lse, query_mask, qkv_rows, key_masks[0], prior, True, True
    )
    grad_k = sum([part[0].astype(jnp.float32) for part in returned], grad_k.astype(jnp.float32))
    grad_v = sum([part[1].astype(jnp.float32) for part in returned], grad_v.astype(jnp.float32))
    grad_qkv = jnp.concatenate(
        [grad_q, grad_k.astype(jnp.bfloat16), grad_v.astype(jnp.bfloat16)], axis=1
    )
    d_qkv_bias = jnp.sum(grad_qkv.astype(jnp.float32), axis=0)
    d_qkv = reduce(outer_sum(normed_one_low, grad_qkv))
    grad_norm_one = back_dot(grad_qkv, qkv_w)
    d_gain_attn = jnp.sum(grad_norm_one * unit_one, axis=0)
    d_shift_attn = jnp.sum(grad_norm_one, axis=0)
    grad_x = grad_resid + norm_back(grad_norm_one, unit_one, inv_one, gain_attn)
    token_grad = from_packs(grad_x.astype(jnp.bfloat16))
    vector_grads = (
        d_gain_attn,
        d_shift_attn,
        d_qkv_bias[:width],
        d_qkv_bias[2 * width :],
        d_bias_out,
        d_scale_attn,
        d_gain_mlp,
        d_shift_mlp,
        d_bias_up,
        d_bias_down,
        d_scale_mlp,
    )
    stacked = jnp.concatenate([grad.reshape(devices, -1) for grad in vector_grads], axis=1)
    summed = lax.psum_scatter(stacked, AXES, scatter_dimension=0, tiled=True)[0]
    return (block_out, token_grad, d_qkv, d_out, d_up, d_down) + tuple(
        summed[low:high] for low, high in ends
    )


def solution(mesh):
    rows = P(None, AXES, None)
    column = P(None, "gy", None)
    matrix = P(AXES, None)
    vector = P(AXES)
    return jax.shard_map(
        functools.partial(shards, mesh.shape["gx"], mesh.shape["gy"]),
        mesh=mesh,
        in_specs=(rows, rows, column, column) + (matrix,) * 4 + (vector,) * 11,
        out_specs=(rows, rows) + (matrix,) * 4 + (vector,) * 11,
        check_vma=False,
    )
```

```python
import functools

import jax
import jax.numpy as jnp
from jax import lax
from jax.experimental import pallas as pl
from jax.experimental.pallas import tpu as pltpu
from jax.sharding import PartitionSpec as P

HEAD_DIM = 64
PAIR = 2 * HEAD_DIM
BLOCK = 128
EPS = 1e-06
MASKED = -1e30
ID_LANES = 8
SCALE = HEAD_DIM ** (-0.5)
LOG2E = 1.4426950408889634
EXP_SCALE = SCALE * LOG2E
AXES = ("gx", "gy")
NT = (((1,), (1,)), ((), ()))
NN = (((1,), (0,)), ((), ()))
VMEM_BYTES = 50 * 1024 * 1024


def dot32(left, right, dims):
    return lax.dot_general(left, right, dims, preferred_element_type=jnp.float32)


def norm_parts(rows, gain, shift):
    mean_row = jnp.mean(rows, axis=-1, keepdims=True)
    centered = rows - mean_row
    inv_std = lax.rsqrt(jnp.mean(centered * centered, axis=-1, keepdims=True) + EPS)
    unit_rows = centered * inv_std
    return (unit_rows * gain + shift, unit_rows, inv_std)


def norm_back(grad_out, unit_rows, inv_std, gain):
    scaled = grad_out * gain
    return inv_std * (
        scaled
        - jnp.mean(scaled, axis=-1, keepdims=True)
        - unit_rows * jnp.mean(scaled * unit_rows, axis=-1, keepdims=True)
    )


def outer_sum(left, right):
    return dot32(left, right, (((0,), (0,)), ((), ())))


def back_dot(grad_rows, weight):
    return dot32(grad_rows, weight, NT)


def lane_of(shape):
    return lax.broadcasted_iota(jnp.int32, shape, len(shape) - 1)


def attend_kernel(group, *refs):
    q_ref, qmask_ref = refs[:2]
    k_refs = refs[2 : 2 + group]
    v_refs = refs[2 + group : 2 + 2 * group]
    mask_refs = refs[2 + 2 * group : 2 + 3 * group]
    out_ref, lse_ref = refs[2 + 3 * group :]
    q = q_ref[...].astype(jnp.float32)
    qmask = qmask_ref[...].astype(jnp.float32)
    first = lane_of(q.shape) < HEAD_DIM
    key_first = lane_of(k_refs[0].shape) < HEAD_DIM
    accs, tops = [], []
    for head in range(2):
        q_head = jnp.where(first == (head == 0), q, qmask).astype(jnp.bfloat16)
        mine = key_first == (head == 0)
        scores = []
        for k_ref, mask_ref in zip(k_refs, mask_refs):
            k_head = jnp.where(
                mine, k_ref[...].astype(jnp.float32), mask_ref[...].astype(jnp.float32)
            ).astype(jnp.bfloat16)
            scores.append(dot32(q_head, k_head, NT))
        top = functools.reduce(
            jnp.maximum, [jnp.max(score, axis=-1, keepdims=True) for score in scores]
        )
        acc = jnp.zeros(q.shape, jnp.float32)
        for score, v_ref in zip(scores, v_refs):
            weights = jnp.exp2((score - top) * EXP_SCALE).astype(jnp.bfloat16)
            v_head = jnp.where(mine, v_ref[...].astype(jnp.float32), 1.0).astype(jnp.bfloat16)
            acc = acc + dot32(weights, v_head, NN)
        accs.append(acc)
        tops.append(top)
    mixed = jnp.where(first, accs[0], accs[1])
    sums = jnp.where(first, accs[1], accs[0])
    out_ref[...] = (mixed / pltpu.roll(sums, HEAD_DIM, 1)).astype(out_ref.dtype)
    lse_ref[...] = jnp.where(first, tops[1], tops[0]) + jnp.log2(sums) * (1.0 / EXP_SCALE)


def attend(qkv_rows, others, query_mask, key_masks):
    rows, width = qkv_rows.shape[0], qkv_rows.shape[1] // 3
    pairs = width // PAIR
    tile = rows // 2
    group = 1 + len(others)

    def col(offset):
        return pl.BlockSpec((rows, PAIR), lambda j, i: (0, offset * pairs + j))

    whole = pl.BlockSpec((rows, PAIR), lambda j, i: (0, 0))
    tiled = pl.BlockSpec((tile, PAIR), lambda j, i: (i, j))
    cells = 2 * pairs * rows * rows * group
    return pl.pallas_call(
        functools.partial(attend_kernel, group),
        grid=(pairs, 2),
        in_specs=[tiled, pl.BlockSpec((tile, PAIR), lambda j, i: (i, 0))]
        + [col(1)]
        + [col(0)] * (group - 1)
        + [col(2)]
        + [col(1)] * (group - 1)
        + [whole] * group,
        out_specs=[tiled, tiled],
        out_shape=[
            jax.ShapeDtypeStruct((rows, width), jnp.bfloat16),
            jax.ShapeDtypeStruct((rows, width), jnp.float32),
        ],
        compiler_params=pltpu.CompilerParams(vmem_limit_bytes=VMEM_BYTES),
        cost_estimate=pl.CostEstimate(
            flops=cells * 512, bytes_accessed=rows * width * 16, transcendentals=cells
        ),
        name="attend",
    )(qkv_rows, query_mask, qkv_rows, *others, qkv_rows, *others, *key_masks)


def back_kernel(has_prior, *refs):
    q_ref, g_ref, o_ref, lse_ref, qmask_ref, k_ref, v_ref, kmask_ref = refs[:8]
    prior_ref = refs[8] if has_prior else None
    dq_ref, dk_ref, dv_ref = refs[8 + has_prior :]
    q_low, g_low, k_low = q_ref[...], g_ref[...], k_ref[...]
    q = q_low.astype(jnp.float32)
    g = g_low.astype(jnp.float32)
    k = k_low.astype(jnp.float32)
    v = v_ref[...].astype(jnp.float32)
    qmask = qmask_ref[...].astype(jnp.float32)
    kmask = kmask_ref[...].astype(jnp.float32)
    lse = lse_ref[...]
    product = g * o_ref[...].astype(jnp.float32)
    lane = lane_of(q.shape)
    first = lane < HEAD_DIM
    spare = lane % HEAD_DIM
    key_lane = lane_of(k.shape)
    key_first = key_lane < HEAD_DIM
    key_spare = key_lane % HEAD_DIM
    ones = (key_spare >= ID_LANES) & (key_spare < ID_LANES + 3)
    key_fill = jnp.where(ones, -1.0, kmask)
    value_fill = jnp.where(ones, -1.0, 0.0)
    k_turned = k.T.astype(jnp.bfloat16)

    def split(values, rest):
        high = values.astype(jnp.bfloat16).astype(jnp.float32)
        left = values - high
        middle = left.astype(jnp.bfloat16).astype(jnp.float32)
        low = left - middle
        return jnp.where(
            spare == ID_LANES,
            high,
            jnp.where(
                spare == ID_LANES + 1, middle, jnp.where(spare == ID_LANES + 2, low, rest)
            ),
        )

    query_fill = split(lse, qmask)
    delta = [
        jnp.sum(jnp.where(first == (head == 0), product, 0.0), axis=-1, keepdims=True)
        for head in range(2)
    ]
    grad_fill = split(jnp.where(first, delta[1], delta[0]), 0.0)
    dq_turned, dks, dvs = [], [], []
    for head in range(2):
        mine = first == (head == 0)
        key_mine = key_first == (head == 0)
        q_head = jnp.where(mine, q, query_fill).astype(jnp.bfloat16)
        g_head = jnp.where(mine, g, grad_fill).astype(jnp.bfloat16)
        k_head = jnp.where(key_mine, k, key_fill).astype(jnp.bfloat16)
        v_head = jnp.where(key_mine, v, value_fill).astype(jnp.bfloat16)
        probs = jnp.exp2(dot32(k_head, q_head, NT) * EXP_SCALE)
        grads = (probs * dot32(v_head, g_head, NT)).astype(jnp.bfloat16)
        dvs.append(dot32(probs.astype(jnp.bfloat16), g_low, NN))
        dks.append(dot32(grads, q_low, NN))
        dq_turned.append(
            dot32(k_turned[head * HEAD_DIM : (head + 1) * HEAD_DIM], grads, NN)
        )
    dq = jnp.concatenate(dq_turned, axis=0).T * SCALE
    if has_prior:
        dq = dq + prior_ref[...]
    dq_ref[...] = dq.astype(dq_ref.dtype)
    dk_ref[...] = (jnp.where(key_first, dks[0], dks[1]) * SCALE).astype(dk_ref.dtype)
    dv_ref[...] = jnp.where(key_first, dvs[0], dvs[1]).astype(dv_ref.dtype)


def attend_back(
    qkv_rows, grad_mixed, mixed, lse, query_mask, key_value, key_mask, prior, own, last
):
    rows, width = mixed.shape
    pairs = width // PAIR

    def col(offset):
        return pl.BlockSpec((rows, PAIR), lambda j: (0, offset * pairs + j))

    whole = pl.BlockSpec((rows, PAIR), lambda j: (0, 0))
    has_prior = prior is not None
    cells = 2 * pairs * rows * rows
    return pl.pallas_call(
        functools.partial(back_kernel, has_prior),
        grid=(pairs,),
        in_specs=[col(0)] * 4
        + [whole, col(1 if own else 0), col(2 if own else 1), whole]
        + [col(0)] * has_prior,
        out_specs=[col(0)] * 3,
        out_shape=[
            jax.ShapeDtypeStruct((rows, width), jnp.bfloat16 if last else jnp.float32),
            jax.ShapeDtypeStruct((rows, width), jnp.bfloat16),
            jax.ShapeDtypeStruct((rows, width), jnp.bfloat16),
        ],
        compiler_params=pltpu.CompilerParams(vmem_limit_bytes=VMEM_BYTES),
        cost_estimate=pl.CostEstimate(
            flops=cells * 1280, bytes_accessed=rows * width * 20, transcendentals=cells
        ),
        name="attend_back",
    )(
        qkv_rows,
        grad_mixed,
        mixed,
        lse,
        query_mask,
        key_value,
        key_value,
        key_mask,
        *([prior] if has_prior else []),
    )


def gelu_parts(values):
    phi = 0.5 * (1.0 + lax.erf(values * 0.7071067811865476))
    density = 0.3989422804014327 * jnp.exp(-0.5 * values * values)
    return values * phi, phi + values * density


def shards(n_gx, n_gy, tokens, cotangent, image_ids, block_layout, *params):
    qkv_weight, out_weight, up_weight, down_weight = params[:4]
    vectors = params[4:]
    devices = n_gx * n_gy
    chips = n_gx // 4
    group = 2 * chips
    row_count, width = tokens.shape[1:]
    place = lax.axis_index("gx")
    odd = place % 2 == 1

    def linear(line, pack, member):
        return (pack * chips + member // 2) * n_gy + 2 * line + member % 2

    moves = [
        [
            (z * n_gy + 2 * line + core, linear(line, 2 * ((step + z) % 2) + core, z // 2))
            for z in range(n_gx)
            for line in range(n_gy // 2)
            for core in range(2)
        ]
        for step in range(2)
    ]
    rounds = [
        [
            (linear(line, pack, member), linear(line, pack, (member + turn) % group))
            for line in range(n_gy // 2)
            for pack in range(4)
            for member in range(group)
        ]
        for turn in range(1, group)
    ]

    def back(perm):
        return [(target, source) for source, target in perm]

    def to_packs(pair):
        even_first = [jnp.where(odd, pair[1], pair[0]), jnp.where(odd, pair[0], pair[1])]
        return jnp.concatenate(
            [lax.ppermute(part, AXES, moves[step]) for step, part in enumerate(even_first)],
            axis=0,
        )

    def from_packs(rows):
        parts = [
            lax.ppermute(
                rows[step * row_count : (step + 1) * row_count], AXES, back(moves[step])
            )
            for step in range(2)
        ]
        return jnp.stack(
            [jnp.where(odd, parts[1], parts[0]), jnp.where(odd, parts[0], parts[1])]
        )

    def gather(shard):
        return lax.all_gather(shard, AXES, axis=0, tiled=True)

    blocks = row_count // BLOCK
    own_layout = lax.dynamic_slice_in_dim(block_layout[:, 0], place * blocks, blocks, axis=1)
    own_ids = jnp.take_along_axis(
        image_ids[:, 0].reshape(image_ids.shape[0], -1, BLOCK), own_layout[..., None], axis=1
    ).reshape(-1, row_count)

    x_low = to_packs(tokens)
    sizes = [vector.shape[0] for vector in vectors]
    fetched = gather(jnp.concatenate(vectors)[None])
    ends, start = [], 0
    for size in sizes:
        ends.append((start, start + size))
        start += size
    (
        gain_attn,
        shift_attn,
        bias_query,
        bias_value,
        bias_out,
        scale_attn,
        gain_mlp,
        shift_mlp,
        bias_up,
        bias_down,
        scale_mlp,
    ) = [fetched[:, low:high].reshape(-1).astype(jnp.float32) for low, high in ends]
    shard_rows = qkv_weight.shape[0]
    merged = gather(
        jnp.concatenate(
            [qkv_weight, out_weight, up_weight, down_weight.reshape(shard_rows, -1)], axis=1
        )
    )
    cuts = [3 * width, 4 * width, 8 * width]
    qkv_w = merged[:, : cuts[0]]
    out_w = merged[:, cuts[0] : cuts[1]]
    up_w = merged[:, cuts[1] : cuts[2]]
    down_w = merged[:, cuts[2] :].reshape(-1, width)

    ids = to_packs(own_ids)
    id_sets = [ids] + [lax.ppermute(ids, AXES, perm) for perm in rounds]
    spare = jnp.arange(PAIR, dtype=jnp.int32)[None, :] % HEAD_DIM
    query_mask = (spare == ids[:, None]).astype(jnp.bfloat16)
    key_masks = [
        jnp.where((spare < ID_LANES) & (spare != each[:, None]), MASKED, 0.0).astype(jnp.bfloat16)
        for each in id_sets
    ]

    x_rows = x_low.astype(jnp.float32)
    normed_one, unit_one, inv_one = norm_parts(x_rows, gain_attn, shift_attn)
    normed_one_low = normed_one.astype(jnp.bfloat16)
    qkv_bias = jnp.concatenate([bias_query, jnp.zeros_like(bias_query), bias_value])
    qkv_rows = (
        jnp.dot(normed_one_low, qkv_w, preferred_element_type=jnp.float32) + qkv_bias
    ).astype(jnp.bfloat16)
    own_kv = qkv_rows[:, width:]
    others = [lax.ppermute(own_kv, AXES, perm) for perm in rounds]
    mixed_low, lse = attend(qkv_rows, others, query_mask, key_masks)
    branch_one = jnp.dot(mixed_low, out_w, preferred_element_type=jnp.float32) + bias_out
    resid = x_rows + scale_attn * branch_one
    normed_two, unit_two, inv_two = norm_parts(resid, gain_mlp, shift_mlp)
    normed_two_low = normed_two.astype(jnp.bfloat16)
    hidden = jnp.dot(normed_two_low, up_w, preferred_element_type=jnp.float32) + bias_up
    active, slope = gelu_parts(hidden)
    active_low = active.astype(jnp.bfloat16)
    branch_two = jnp.dot(active_low, down_w, preferred_element_type=jnp.float32) + bias_down
    block_out = from_packs((resid + scale_mlp * branch_two).astype(jnp.bfloat16))

    def reduce(total):
        return lax.psum_scatter(
            total.astype(jnp.bfloat16), AXES, scatter_dimension=0, tiled=True
        ).astype(jnp.float32)

    grad_y = to_packs(cotangent).astype(jnp.float32)
    d_scale_mlp = jnp.sum(grad_y * branch_two, axis=0)
    grad_two = (scale_mlp * grad_y).astype(jnp.bfloat16)
    d_bias_down = jnp.sum(grad_two.astype(jnp.float32), axis=0)
    sum_down = outer_sum(active_low, grad_two).astype(jnp.bfloat16)
    grad_hidden = (back_dot(grad_two, down_w) * slope).astype(jnp.bfloat16)
    d_bias_up = jnp.sum(grad_hidden.astype(jnp.float32), axis=0)
    sum_up = outer_sum(normed_two_low, grad_hidden).astype(jnp.bfloat16)
    grad_norm_two = back_dot(grad_hidden, up_w)
    d_gain_mlp = jnp.sum(grad_norm_two * unit_two, axis=0)
    d_shift_mlp = jnp.sum(grad_norm_two, axis=0)
    grad_resid = grad_y + norm_back(grad_norm_two, unit_two, inv_two, gain_mlp)
    d_scale_attn = jnp.sum(grad_resid * branch_one, axis=0)
    grad_one = (scale_attn * grad_resid).astype(jnp.bfloat16)
    d_bias_out = jnp.sum(grad_one.astype(jnp.float32), axis=0)
    sum_out = outer_sum(mixed_low, grad_one).astype(jnp.bfloat16)
    early = reduce(jnp.concatenate([sum_out, sum_up, sum_down.reshape(width, -1)], axis=1))
    d_out = early[:, :width]
    d_up = early[:, width : 5 * width]
    d_down = early[:, 5 * width :].reshape(down_weight.shape)
    grad_mixed = back_dot(grad_one, out_w).astype(jnp.bfloat16)

    prior, returned = None, []
    for perm, key_value, key_mask in zip(rounds, others, key_masks[1:]):
        prior, part_k, part_v = attend_back(
            qkv_rows, grad_mixed, mixed_low, lse, query_mask, key_value, key_mask, prior, False, False
        )
        returned.append(
            (lax.ppermute(part_k, AXES, back(perm)), lax.ppermute(part_v, AXES, back(perm)))
        )
    grad_q, grad_k, grad_v = attend_back(
        qkv_rows, grad_mixed, mixed_low, lse, query_mask, qkv_rows, key_masks[0], prior, True, True
    )
    grad_k = sum([part[0].astype(jnp.float32) for part in returned], grad_k.astype(jnp.float32))
    grad_v = sum([part[1].astype(jnp.float32) for part in returned], grad_v.astype(jnp.float32))
    grad_qkv = jnp.concatenate(
        [grad_q, grad_k.astype(jnp.bfloat16), grad_v.astype(jnp.bfloat16)], axis=1
    )
    d_qkv_bias = jnp.sum(grad_qkv.astype(jnp.float32), axis=0)
    d_qkv = reduce(outer_sum(normed_one_low, grad_qkv))
    grad_norm_one = back_dot(grad_qkv, qkv_w)
    d_gain_attn = jnp.sum(grad_norm_one * unit_one, axis=0)
    d_shift_attn = jnp.sum(grad_norm_one, axis=0)
    grad_x = grad_resid + norm_back(grad_norm_one, unit_one, inv_one, gain_attn)
    token_grad = from_packs(grad_x.astype(jnp.bfloat16))
    vector_grads = (
        d_gain_attn,
        d_shift_attn,
        d_qkv_bias[:width],
        d_qkv_bias[2 * width :],
        d_bias_out,
        d_scale_attn,
        d_gain_mlp,
        d_shift_mlp,
        d_bias_up,
        d_bias_down,
        d_scale_mlp,
    )
    stacked = jnp.concatenate([grad.reshape(devices, -1) for grad in vector_grads], axis=1)
    summed = lax.psum_scatter(stacked, AXES, scatter_dimension=0, tiled=True)[0]
    return (block_out, token_grad, d_qkv, d_out, d_up, d_down) + tuple(
        summed[low:high] for low, high in ends
    )


def solution(mesh):
    rows = P(None, AXES, None)
    column = P(None, "gy", None)
    matrix = P(AXES, None)
    vector = P(AXES)
    return jax.shard_map(
        functools.partial(shards, mesh.shape["gx"], mesh.shape["gy"]),
        mesh=mesh,
        in_specs=(rows, rows, column, column) + (matrix,) * 4 + (vector,) * 11,
        out_specs=(rows, rows) + (matrix,) * 4 + (vector,) * 11,
        check_vma=False,
    )
```
